32 devices in a mesh: seg: 8 (over y, x, core), head: 4 (over z).
Axes of the slice: x: 2, y: 2, z: 4, core: 2. Of those that a mesh axis runs over, the one named last changes fastest.
Arguments:
- tokens: float32 [4096, 2048], P(('seg', 'head'))
- document_index: int32 [4096], P('seg'), may hold values from 0 to 31, never falling along the last dimension, each value on 1 to 256 neighbouring positions
- block_mask: int32 [8, 4, 4], P('seg'), may hold values from 0 to 1, as said below
- slot_keys: bfloat16 [2, 128, 2048], P(None, None, 'head'), may hold values from -8 to 8
- mem_init: float32 [2, 128, 2048], P(None, None, 'head'), may hold values from -6 to 6
- retain: float32 [2, 8, 32], P(None, 'seg', 'head'), may hold values from 0.005 to 1
- attn_gain: float32 [2, 2048], replicated, may hold values from 0.25 to 4
- mlp_gain: float32 [2, 2048], replicated, may hold values from 0.25 to 4
- w_query: bfloat16 [2, 2048, 2048], P(None, None, 'head')
- w_kv: bfloat16 [2, 2048, 1024], P(None, None, 'head')
- w_out: bfloat16 [2, 2048, 2048], P(None, 'head'), may hold values from -0.125 to 0.125
- w_gate_up: bfloat16 [2, 2048, 2, 4096], P(None, None, None, 'head'), may hold values from -0.125 to 0.125
- w_down: bfloat16 [2, 4096, 2048], P(None, 'head'), may hold values from -0.09375 to 0.09375
Outputs:
- hidden: float32 [4096, 2048], P(('seg', 'head'))
- memory: float32 [2, 8, 128, 2048], P(None, 'seg', None, 'head')
The draws below stay inside these ranges and needn't reach their ends.
Inputs may be any that keep to these rules, and one draw needn't show every extreme that they name: `document_index`: document numbers never fall along the sequence. `block_mask`: in every segment the blocks on the diagonal are 1 and the blocks above it 0.
All inputs are finite; a program needn't handle non-finite values.
Results may differ from the reference program's by a relative error of at most 0.025.
Values may be sent and summed in bfloat16 or wider, within the bound.
A program may use at most 192 MiB of HBM per device.

```python
import math
import jax
import jax.numpy as jnp
import numpy as np
from jax import lax

D = 2048
HEADS = 32
KV_HEADS = 8
HD = 64
FF = 4096
MEM = 128
SEG_LEN = 512
BLOCK = 128
DEPTH_NUMBER = 2
PIECE_NUMBER = 8
SEQ = 4096


def draw_tokens(key, part):
    first_key = jax.random.fold_in(key, 0)
    return jax.random.normal(first_key, (SEQ, D), jnp.float32)


def draw_block_mask(key, part):
    count = SEG_LEN // BLOCK
    bits = jax.random.randint(key, (PIECE_NUMBER, count, count), 0, 2)
    row_at = jnp.arange(count)[:, None]
    col_at = jnp.arange(count)[None, :]
    return jnp.where(row_at == col_at, 1, jnp.where(row_at > col_at, bits, 0)).astype(jnp.int32)


def draw_slot_keys(key, part):
    base = jax.random.fold_in(key, 29)
    entry_key = jax.random.fold_in(base, 0)
    entries = jax.random.normal(entry_key, (DEPTH_NUMBER, MEM, HEADS * HD), jnp.float32)
    return jnp.clip(entries, -4.0, 4.0).astype(jnp.bfloat16)


def draw_retain(key, part):
    lookup_vectors = jax.random.split(key, 5)
    share = 0.5
    pick = jax.random.uniform(lookup_vectors[0], (DEPTH_NUMBER, 1, HEADS), jnp.float32)
    fast = jax.random.uniform(lookup_vectors[1], (DEPTH_NUMBER, PIECE_NUMBER, HEADS), jnp.float32, 0.03, 0.3)
    gradual_memory = jnp.exp(jnp.log(0.1) * jax.random.uniform(lookup_vectors[2], (DEPTH_NUMBER, PIECE_NUMBER, HEADS), jnp.float32, 0.1, 0.6) / PIECE_NUMBER)
    symbol_group = jax.random.uniform(lookup_vectors[3], (DEPTH_NUMBER, PIECE_NUMBER, 1), jnp.float32) < 2.5 / PIECE_NUMBER
    split_location = jax.random.uniform(lookup_vectors[4], (DEPTH_NUMBER, PIECE_NUMBER, HEADS), jnp.float32, 0.5, 0.8)
    gradual_memory = jnp.where(symbol_group, gradual_memory * split_location, gradual_memory)
    return jnp.where(pick < share, fast, gradual_memory).astype(jnp.float32)


def projections(key):
    base = jax.random.fold_in(key, 17)
    query_key, pair_key = jax.random.split(base, 2)
    factor = D ** (-0.5)
    pair_weight = jax.random.normal(pair_key, (DEPTH_NUMBER, D, KV_HEADS * 2 * HD), jnp.float32) * factor
    query_weight = jax.random.normal(query_key, (DEPTH_NUMBER, D, HEADS * HD), jnp.float32) * factor
    return (query_weight, pair_weight)


def draw_w_query(key, part):
    return projections(key)[0].astype(jnp.bfloat16)


def draw_w_kv(key, part):
    return projections(key)[1].astype(jnp.bfloat16)


def levels(rng, dims, cuts, smallest, top_value):
    loudness = 1.0
    for dim, blocks in cuts:
        draws = jax.random.uniform(jax.random.fold_in(jax.random.fold_in(rng, 6), dim), (blocks,), jnp.float32, smallest / len(cuts), top_value / len(cuts))
        loudness = loudness * jnp.repeat(jnp.exp(draws), dims[dim] // blocks).reshape((-1,) + (1,) * (len(dims) - 1 - dim))
    return loudness


def length_profile(count, total, bound, skew):
    loads = [(1 << 20) // math.isqrt(rank ** skew) + 1 for rank in range(2, count + 1)]
    surplus, counts = total - bound - (count - 1), [1] * (count - 1)
    while surplus > 0:
        free = [i for i in range(count - 1) if counts[i] < bound]
        whole, left = sum([loads[i] for i in free]), surplus
        for i in free:
            addition = min(bound - counts[i], max(1, left * loads[i] // whole), surplus)
            counts[i] = counts[i] + addition
            surplus = surplus - addition
    return np.array([bound] + counts)


def ragged(own_key, number_of, total, most, skew):
    if number_of == 2:
        one = jax.random.randint(own_key, (), max(1, total - most), min(most, total - 1) + 1)
        return jnp.stack([one, total - one])
    lengths = jnp.asarray(length_profile(number_of, total, most, skew), jnp.int32)
    twos = (number_of - 1) // 2
    giver, sink = lengths[1:1 + 2 * twos:2], lengths[2:2 + 2 * twos:2]
    room = jnp.minimum(giver - 1, most - sink)
    passed = jax.random.randint(jax.random.fold_in(own_key, 1), (twos,), 0, 1 << 20) % (room + 1)
    lengths = lengths.at[1:1 + 2 * twos:2].set(giver - passed).at[2:2 + 2 * twos:2].set(sink + passed)
    return lengths[jax.random.permutation(jax.random.fold_in(own_key, 2), number_of)]


def centred(own_key, dims, spread, limit, cuts=(), held_as=jnp.bfloat16):
    values = spread * jax.random.normal(own_key, dims, jnp.float32)
    if cuts:
        values = values * levels(own_key, dims, cuts, -0.22, 0.18)
    return jnp.clip(values, -limit, limit).astype(held_as)


def setup_inputs(seed: int = 0) -> dict:
    keys = jax.random.split(jax.random.key(seed), 14)
    tokens = draw_tokens(jax.random.fold_in(keys[13], 71), 0)
    document_index = jnp.searchsorted(jnp.cumsum(ragged(keys[1], 4 * PIECE_NUMBER, SEQ, SEG_LEN // 2, 2)), jnp.arange(SEQ), side="right").astype(jnp.int32)
    block_mask = draw_block_mask(jax.random.fold_in(keys[13], 71), 0)
    slot_keys = draw_slot_keys(jax.random.fold_in(keys[13], 71), 0)
    mem_init = centred(keys[4], (DEPTH_NUMBER, MEM, HEADS * HD), 1.0, 6.0, ((2, 4),), jnp.float32)
    retain = draw_retain(jax.random.fold_in(keys[13], 71), 0)
    attn_gain = jnp.clip(jnp.exp(jax.random.uniform(keys[6], (DEPTH_NUMBER, D), jnp.float32, math.log(0.25), math.log(4.0))), 0.25, 4.0)
    mlp_gain = jnp.clip(jnp.exp(jax.random.uniform(keys[7], (DEPTH_NUMBER, D), jnp.float32, math.log(0.25), math.log(4.0))), 0.25, 4.0)
    w_query = draw_w_query(jax.random.fold_in(keys[13], 71), 0)
    w_kv = draw_w_kv(jax.random.fold_in(keys[13], 71), 0)
    w_out = centred(keys[10], (DEPTH_NUMBER, HEADS * HD, D), (HEADS * HD) ** -0.5, 0.125, ((1, 4),))
    w_gate_up = centred(keys[11], (DEPTH_NUMBER, D, 2, FF), D ** -0.5, 0.125, ((3, 4),))
    w_down = centred(keys[12], (DEPTH_NUMBER, FF, D), FF ** -0.5, 0.09375, ((1, 4),))
    return dict(tokens=tokens, document_index=document_index, block_mask=block_mask, slot_keys=slot_keys, mem_init=mem_init, retain=retain, attn_gain=attn_gain, mlp_gain=mlp_gain, w_query=w_query, w_kv=w_kv, w_out=w_out, w_gate_up=w_gate_up, w_down=w_down)


def rounded(value):
    return lax.optimization_barrier(value.astype(jnp.bfloat16)).astype(jnp.float32)

def rms_norm(value, gain):
    wide = value.astype(jnp.float32)
    factor = lax.rsqrt(lax.optimization_barrier(jnp.mean(wide * wide, axis=-1, keepdims=True)) + 1e-05)
    return (wide * factor * gain).astype(jnp.bfloat16)

def rope_tables(position):
    half = HD // 2
    freq = 500000.0 ** (-(jnp.arange(half).astype(jnp.float32) * 2.0 / HD))
    angle = position.astype(jnp.float32)[:, None] * freq[None, :]
    return (jnp.cos(angle), jnp.sin(angle))

def rotate(tensor, cosine, sine):
    half = tensor.shape[-1] // 2
    first = tensor[..., :half]
    second = tensor[..., half:]
    cos_part = cosine[:, None, :]
    sin_part = sine[:, None, :]
    return jnp.concatenate([first * cos_part - second * sin_part, second * cos_part + first * sin_part], axis=-1)

def reference(tokens, document_index, block_mask, slot_keys, mem_init, retain, attn_gain, mlp_gain, w_query, w_kv, w_out, w_gate_up, w_down):
    group = HEADS // KV_HEADS
    scale = HD ** (-0.5)
    cosine, sine = rope_tables(jnp.arange(SEQ) % SEG_LEN)
    docs = document_index.reshape(PIECE_NUMBER, SEG_LEN)
    causal = jnp.arange(SEG_LEN)[:, None] >= jnp.arange(SEG_LEN)[None, :]
    stream = tokens
    stored = []
    for layer in range(DEPTH_NUMBER):
        normed = rms_norm(stream, attn_gain[layer])
        query = jnp.dot(normed, w_query[layer], preferred_element_type=jnp.float32)
        pairs = jnp.dot(normed, w_kv[layer], preferred_element_type=jnp.float32).reshape(SEQ, KV_HEADS, 2, HD)
        query = rotate(query.reshape(SEQ, HEADS, HD), cosine, sine).astype(jnp.bfloat16).reshape(PIECE_NUMBER, SEG_LEN, KV_HEADS, group, HD)
        lookup_vectors = rotate(pairs[:, :, 0], cosine, sine).astype(jnp.bfloat16).reshape(PIECE_NUMBER, SEG_LEN, KV_HEADS, HD)
        values = pairs[:, :, 1].astype(jnp.bfloat16).reshape(PIECE_NUMBER, SEG_LEN, KV_HEADS, HD)
        slots = slot_keys[layer].reshape(MEM, KV_HEADS, group, HD).astype(jnp.float32)

        def write_one(inputs):
            seg_keys, seg_values = inputs
            scores = jnp.einsum('mkgd,jkd->kgmj', slots, seg_keys.astype(jnp.float32)) * scale
            probs = rounded(jax.nn.softmax(scores, axis=-1))
            return jnp.einsum('kgmj,jkd->mkgd', probs, seg_values.astype(jnp.float32)).reshape(MEM, HEADS * HD)
        written = lax.map(write_one, (lookup_vectors, values))
        rates = jnp.repeat(retain[layer], HD, axis=1)[:, None, :]

        def advance(state, inputs):
            rate, fresh = inputs
            after = rate * state + (1.0 - rate) * fresh
            return (after, (state, after))
        final_state, (before, after) = lax.scan(advance, mem_init[layer], (rates, written))
        stored.append(after)

        def fetch_single(inputs):
            seg_query, seg_keys, seg_values, memory_state, seg_docs, seg_blocks = inputs
            blocks = jnp.repeat(jnp.repeat(seg_blocks, BLOCK, axis=0), BLOCK, axis=1)
            allowed = causal & (seg_docs[:, None] == seg_docs[None, :]) & (blocks == 1)
            query_wide = seg_query.astype(jnp.float32)
            slot_scores = jnp.einsum('ikgd,mkgd->kgim', query_wide, slots) * scale
            token_scores = jnp.einsum('ikgd,jkd->kgij', query_wide, seg_keys.astype(jnp.float32)) * scale
            token_scores = jnp.where(allowed, token_scores, -jnp.inf)
            probs = rounded(jax.nn.softmax(jnp.concatenate([slot_scores, token_scores], axis=-1), axis=-1))
            memory_read = rounded(memory_state).reshape(MEM, KV_HEADS, group, HD)
            result = jnp.einsum('kgim,mkgd->ikgd', probs[..., :MEM], memory_read)
            result = result + jnp.einsum('kgij,jkd->ikgd', probs[..., MEM:], seg_values.astype(jnp.float32))
            return result.reshape(SEG_LEN, HEADS * HD).astype(jnp.bfloat16)
        attended = lax.map(fetch_single, (query, lookup_vectors, values, before, docs, block_mask)).reshape(SEQ, HEADS * HD)
        mixed = jnp.dot(attended, w_out[layer], preferred_element_type=jnp.float32)
        middle = stream + mixed
        normed = rms_norm(middle, mlp_gain[layer])
        gate = jnp.dot(normed, w_gate_up[layer][:, 0], preferred_element_type=jnp.float32)
        upper = jnp.dot(normed, w_gate_up[layer][:, 1], preferred_element_type=jnp.float32)
        inner = (jax.nn.silu(gate) * upper).astype(jnp.bfloat16)
        down = jnp.dot(inner, w_down[layer], preferred_element_type=jnp.float32)
        stream = middle + down
    return (stream, jnp.stack(stored))
```

```python
import functools

import jax
import jax.numpy as jnp
import numpy as np
from jax import lax
from jax.experimental import pallas as pl
from jax.experimental.pallas import tpu as pltpu
from jax.sharding import PartitionSpec as P

HEADS = 32
KV_HEADS = 8
HD = 64
MEM = 128
SEG_LEN = 512
BLOCK = 128
DEPTH_NUMBER = 2
CHUNK = 32
LAG = 4
MESH = pl.DeviceIdType.MESH
F32 = jnp.float32
BF16 = jnp.bfloat16


def enter(me, n):
    barrier = pltpu.get_barrier_semaphore()

    @pl.when(me > 0)
    def _():
        pl.semaphore_signal(barrier, inc=1, device_id={"head": me - 1}, device_id_type=MESH)

    @pl.when(me < n - 1)
    def _():
        pl.semaphore_signal(barrier, inc=1, device_id={"head": me + 1}, device_id_type=MESH)

    @pl.when((me > 0) & (me < n - 1))
    def _():
        pl.semaphore_wait(barrier, 2)

    @pl.when((me == 0) | (me == n - 1))
    def _():
        pl.semaphore_wait(barrier, 1)


def remote(source, target, send, recv, to):
    return pltpu.make_async_remote_copy(
        src_ref=source,
        dst_ref=target,
        send_sem=send,
        recv_sem=recv,
        device_id={"head": to},
        device_id_type=MESH,
    )


def normed_rows(value, gain):
    factor = lax.rsqrt(jnp.mean(value * value, axis=-1, keepdims=True) + 1e-05)
    return (value * factor * gain).astype(BF16)


def rope_lanes(value, cosine, sine):
    lane = lax.broadcasted_iota(jnp.int32, value.shape, 1)
    turned = jnp.where(lane % HD < HD // 2, pltpu.roll(value, 96, 1), pltpu.roll(value, 32, 1))
    return value * cosine + turned * sine


def project_rows(rows, x, wq, wkv, tables, q_out, kv_out):
    cosine, sine, cosine_kv, sine_kv = (table[rows, :] for table in tables)
    block = x[rows, :]
    query = jnp.dot(block, wq[...], preferred_element_type=F32)
    for at in range(0, query.shape[1], 128):
        q_out[rows, at : at + 128] = rope_lanes(query[:, at : at + 128], cosine, sine).astype(BF16)
    pairs = jnp.dot(block, wkv[...], preferred_element_type=F32)
    for at in range(0, pairs.shape[1], 128):
        kv_out[rows, at : at + 128] = rope_lanes(
            pairs[:, at : at + 128], cosine_kv, sine_kv
        ).astype(BF16)


def widen_rows(rows, x, w, out):
    block = x[rows, :]
    tile = 256

    def step(i, carry):
        cols = pl.ds(pl.multiple_of(i * tile, tile), tile)
        gate = jnp.dot(block, w[0, :, cols], preferred_element_type=F32)
        up = jnp.dot(block, w[1, :, cols], preferred_element_type=F32)
        out[rows, cols] = (gate / (1.0 + jnp.exp(-gate)) * up).astype(BF16)
        return carry

    lax.fori_loop(0, out.shape[1] // tile, step, 0)


def partial_rows(rows, x, w, part):
    block = x[rows, :]
    tile = 512

    def step(i, carry):
        cols = pl.ds(pl.multiple_of(i * tile, tile), tile)
        part[rows, cols] = jnp.dot(block, w[:, cols], preferred_element_type=F32)
        return carry

    lax.fori_loop(0, part.shape[1] // tile, step, 0)


def add_rest(me, n, part, rest):
    held = rest.shape[0]
    if held * n == part.shape[0]:
        rows = pl.ds(pl.multiple_of(me * held, held), held)
        part[rows, :] += rest[...]
    else:

        @pl.when(me == 0)
        def _():
            part[:held, :] += rest[...]

        @pl.when(me == n - 1)
        def _():
            part[held:, :] += rest[...]


def gather_kernel(n, layer, tokens, gain, wq_hbm, wkv_hbm, cos_q, sin_q, cos_kv, sin_kv,
                  q_out, kv_out, x, wq, wkv, load, send, recv):
    me = lax.axis_index("head")
    loads = [
        pltpu.make_async_copy(wq_hbm.at[layer], wq, load.at[0]),
        pltpu.make_async_copy(wkv_hbm.at[layer], wkv, load.at[1]),
    ]
    for copy in loads:
        copy.start()
    mine = tokens.shape[0]
    pieces = mine // CHUNK
    enter(me, n)

    def hop(way, shard, piece):
        rows = pl.ds(pl.multiple_of(shard * mine + piece * CHUNK, CHUNK), CHUNK)
        to = me + 1 if way == 0 else me - 1
        to = jnp.clip(to, 0, n - 1)
        at = shard * pieces + piece
        return remote(x.at[rows], x.at[rows], send.at[way, at], recv.at[way, at], to)

    for piece in range(pieces):
        rows = pl.ds(pl.multiple_of(me * mine + piece * CHUNK, CHUNK), CHUNK)
        x[rows, :] = normed_rows(tokens[piece * CHUNK : (piece + 1) * CHUNK, :], gain[...])

        @pl.when(me < n - 1)
        def _():
            hop(0, me, piece).start()

        @pl.when(me > 0)
        def _():
            hop(1, me, piece).start()

    for copy in loads:
        copy.wait()
    tables = (cos_q, sin_q, cos_kv, sin_kv)

    def project(shard):
        rows = pl.ds(pl.multiple_of(shard * mine, mine), mine)
        project_rows(rows, x, wq, wkv, tables, q_out, kv_out)

    project(me)
    for far in range(1, n):
        for piece in range(pieces):

            @pl.when(me - far >= 0)
            def _():
                hop(0, me - far, piece).wait_recv()

                @pl.when(me < n - 1)
                def _():
                    hop(0, me - far, piece).start()

            @pl.when(me + far < n)
            def _():
                hop(1, me + far, piece).wait_recv()

                @pl.when(me > 0)
                def _():
                    hop(1, me + far, piece).start()

        @pl.when(me - far >= 0)
        def _():
            project(me - far)

        @pl.when(me + far < n)
        def _():
            project(me + far)

    for shard in range(n):
        for piece in range(pieces):

            @pl.when((shard <= me) & (me < n - 1))
            def _():
                hop(0, shard, piece).wait_send()

            @pl.when((shard >= me) & (me > 0))
            def _():
                hop(1, shard, piece).wait_send()


def exchange_kernel(n, layer, wide, *refs):
    me = lax.axis_index("head")
    if wide:
        (x, w_hbm, rest, gain, after_hbm, out, stream,
         part, outgoing, arriving, gathered, w, after, load,
         sum_send, sum_recv, all_send, all_recv) = refs
        loads = [
            pltpu.make_async_copy(w_hbm.at[layer], w, load.at[0]),
            pltpu.make_async_copy(after_hbm, after, load.at[1]),
        ]
    else:
        (x, w_hbm, rest, gain, wq_hbm, wkv_hbm, cos_q, sin_q, cos_kv, sin_kv, q_out, kv_out, stream,
         part, outgoing, arriving, gathered, w, wq, wkv, load,
         sum_send, sum_recv, all_send, all_recv) = refs
        loads = [
            pltpu.make_async_copy(w_hbm.at[layer], w, load.at[0]),
            pltpu.make_async_copy(wq_hbm.at[layer + 1], wq, load.at[1]),
            pltpu.make_async_copy(wkv_hbm.at[layer + 1], wkv, load.at[2]),
        ]
    for copy in loads:
        copy.start()
    half = part.shape[0] // 2
    count = half // CHUNK
    enter(me, n)
    loads[0].wait()
    for block in range(0, half, BLOCK):
        for way in (0, 1):
            partial_rows(pl.ds(way * half + block, BLOCK), x, w, part)
    add_rest(me, n, part, rest)

    def place(way, t):
        return pl.ds(pl.multiple_of(way * half + t * CHUNK, CHUNK), CHUNK)

    def sum_hop(way, t):
        rows = place(way, t)
        to = jnp.clip(me - 1 if way == 0 else me + 1, 0, n - 1)
        return remote(outgoing.at[rows], arriving.at[rows], sum_send.at[way, t],
                      sum_recv.at[way, t], to)

    def all_hop(way, t):
        rows = place(way, t)
        to = jnp.clip(me + 1 if way == 0 else me - 1, 0, n - 1)
        return remote(gathered.at[rows], gathered.at[rows], all_send.at[way, t],
                      all_recv.at[way, t], to)

    ends = ((n - 1, 0), (0, n - 1))

    def add_up(t, carry=0):
        for way in (0, 1):
            first, owner = ends[way]
            rows = place(way, t)

            @pl.when(me == first)
            def _():
                outgoing[rows, :] = part[rows, :].astype(BF16)
                sum_hop(way, t).start()

            @pl.when((me != first) & (me != owner))
            def _():
                sum_hop(way, t).wait_recv()
                outgoing[rows, :] = (part[rows, :] + arriving[rows, :].astype(F32)).astype(BF16)
                sum_hop(way, t).start()

            @pl.when(me == owner)
            def _():
                sum_hop(way, t).wait_recv()
                total = part[rows, :] + arriving[rows, :].astype(F32)
                stream[pl.ds(pl.multiple_of(t * CHUNK, CHUNK), CHUNK), :] = total
                gathered[rows, :] = normed_rows(total, gain[...])
                all_hop(way, t).start()

        return carry

    def hand_on(t, carry=0):
        for way in (0, 1):
            first, owner = ends[way]

            @pl.when(me != owner)
            def _():
                all_hop(way, t).wait_recv()

                @pl.when(me != first)
                def _():
                    all_hop(way, t).start()

        return carry

    def both(t, carry):
        add_up(t)
        hand_on(t - LAG)
        return carry

    def finish(way, block):
        rows = pl.ds(way * half + block * BLOCK, BLOCK)
        if wide:
            widen_rows(rows, gathered, after, out)
        else:
            project_rows(rows, gathered, wq, wkv, (cos_q, sin_q, cos_kv, sin_kv), q_out, kv_out)

    lax.fori_loop(0, LAG, add_up, 0)
    lax.fori_loop(LAG, count, both, 0)
    for copy in loads[1:]:
        copy.wait()
    per = BLOCK // CHUNK
    waiting = [(way, block) for block in range((count - LAG) // per) for way in (0, 1)]
    for t in range(count - LAG, count):
        hand_on(t)
        if waiting:
            finish(*waiting.pop(0))
        if (t + 1) % per == 0:
            waiting += [(way, t // per) for way in (0, 1)]
    for item in waiting:
        finish(*item)

    def drain(t, carry):
        for way in (0, 1):
            first, owner = ends[way]

            @pl.when(me != owner)
            def _():
                sum_hop(way, t).wait_send()

            @pl.when(me != first)
            def _():
                all_hop(way, t).wait_send()

        return carry

    lax.fori_loop(0, count, drain, 0)


def scatter_kernel(n, layer, x, w_hbm, rest, out, part, outgoing, arriving, w, load, send, recv):
    me = lax.axis_index("head")
    copy = pltpu.make_async_copy(w_hbm.at[layer], w, load.at[0])
    copy.start()
    mine = out.shape[0]
    pieces = mine // CHUNK
    enter(me, n)
    copy.wait()
    for shard in range(n):
        partial_rows(pl.ds(shard * mine, mine), x, w, part)
    add_rest(me, n, part, rest)

    def place(at):
        return pl.ds(pl.multiple_of(at * CHUNK, CHUNK), CHUNK)

    def hop(way, at):
        rows = place(at)
        to = jnp.clip(me + 1 if way == 0 else me - 1, 0, n - 1)
        return remote(outgoing.at[way, rows], arriving.at[way, rows], send.at[way, at],
                      recv.at[way, at], to)

    def step(i, carry):
        for way in (0, 1):
            shard = n - 1 - i // pieces if way == 0 else i // pieces
            at = shard * pieces + i % pieces
            rows = place(at)
            ahead = me < shard if way == 0 else me > shard
            edge = me == 0 if way == 0 else me == n - 1

            @pl.when(ahead & edge)
            def _():
                outgoing[way, rows, :] = part[rows, :].astype(BF16)
                hop(way, at).start()

            @pl.when(ahead & jnp.logical_not(edge))
            def _():
                hop(way, at).wait_recv()
                outgoing[way, rows, :] = (
                    part[rows, :] + arriving[way, rows, :].astype(F32)
                ).astype(BF16)
                hop(way, at).start()

        return carry

    lax.fori_loop(0, (n - 1) * pieces, step, 0)
    for piece in range(pieces):
        at = me * pieces + piece
        here = slice(piece * CHUNK, (piece + 1) * CHUNK)
        out[here, :] = part[place(at), :]

        @pl.when(me > 0)
        def _():
            hop(0, at).wait_recv()
            out[here, :] += arriving[0, place(at), :].astype(F32)

        @pl.when(me < n - 1)
        def _():
            hop(1, at).wait_recv()
            out[here, :] += arriving[1, place(at), :].astype(F32)

    def drain(at, carry):
        shard = at // pieces

        @pl.when(me < shard)
        def _():
            hop(0, at).wait_send()

        @pl.when(me > shard)
        def _():
            hop(1, at).wait_send()

        return carry

    lax.fori_loop(0, n * pieces, drain, 0)


VM = pl.BlockSpec(memory_space=pltpu.VMEM)
HB = pl.BlockSpec(memory_space=pl.ANY)


def parameters(number):
    return pltpu.CompilerParams(
        collective_id=number, has_side_effects=True, vmem_limit_bytes=48 * 1024 * 1024
    )


def dma(*shape):
    return pltpu.SemaphoreType.DMA(shape)


def gather_project(n, layer, number, tokens, gain, wq, wkv, tables):
    mine, width = tokens.shape
    rows, cq, ck = mine * n, wq.shape[2], wkv.shape[2]
    return pl.pallas_call(
        functools.partial(gather_kernel, n, layer),
        out_shape=[jax.ShapeDtypeStruct((rows, cq), BF16), jax.ShapeDtypeStruct((rows, ck), BF16)],
        in_specs=[VM, VM, HB, HB] + [VM] * 4,
        out_specs=[VM, VM],
        scratch_shapes=[
            pltpu.VMEM((rows, width), BF16),
            pltpu.VMEM(wq.shape[1:], BF16),
            pltpu.VMEM(wkv.shape[1:], BF16),
            dma(2),
            dma(2, rows // CHUNK),
            dma(2, rows // CHUNK),
        ],
        compiler_params=parameters(number),
        name="gather_project",
    )(tokens, gain, wq, wkv, *tables)


def exchange(n, layer, number, x, w, rest, gain, after, tables=None):
    rows, width = x.shape[0], w.shape[2]
    half = rows // 2
    wide = tables is None
    count = half // CHUNK
    if wide:
        outs = [jax.ShapeDtypeStruct((rows, after[0].shape[2]), BF16)]
        kept = [pltpu.VMEM(after[0].shape, BF16)]
    else:
        outs = [jax.ShapeDtypeStruct((rows, part.shape[2]), BF16) for part in after]
        kept = [pltpu.VMEM(part.shape[1:], BF16) for part in after]
    outs.append(jax.ShapeDtypeStruct((half, width), F32))
    more = () if wide else tables
    return pl.pallas_call(
        functools.partial(exchange_kernel, n, layer, wide),
        out_shape=outs,
        in_specs=[VM, HB, VM, VM] + [HB] * len(after) + [VM] * len(more),
        out_specs=[VM] * len(outs),
        scratch_shapes=[
            pltpu.VMEM((rows, width), F32),
            pltpu.VMEM((rows, width), BF16),
            pltpu.VMEM((rows, width), BF16),
            pltpu.VMEM((rows, width), BF16),
            pltpu.VMEM(w.shape[1:], BF16),
            *kept,
            dma(3),
            dma(2, count),
            dma(2, count),
            dma(2, count),
            dma(2, count),
        ],
        compiler_params=parameters(number),
        name="exchange",
    )(x, w, rest, gain, *after, *more)


def scatter(n, layer, number, x, w, rest):
    rows, width = x.shape[0], w.shape[2]
    return pl.pallas_call(
        functools.partial(scatter_kernel, n, layer),
        out_shape=jax.ShapeDtypeStruct((rows // n, width), F32),
        in_specs=[VM, HB, VM],
        out_specs=VM,
        scratch_shapes=[
            pltpu.VMEM((rows, width), F32),
            pltpu.VMEM((2, rows, width), BF16),
            pltpu.VMEM((2, rows, width), BF16),
            pltpu.VMEM(w.shape[1:], BF16),
            dma(1),
            dma(2, rows // CHUNK),
            dma(2, rows // CHUNK),
        ],
        compiler_params=parameters(number),
        name="scatter",
    )(x, w, rest)


def lane_tables():
    freq = 500000.0 ** (-(np.arange(HD // 2) * 2.0 / HD))
    angle = np.arange(SEG_LEN)[:, None] * freq[None, :]
    c, s = np.cos(angle), np.sin(angle)
    cosine, sine = np.concatenate([c, c], 1), np.concatenate([-s, s], 1)
    tables = (
        np.concatenate([cosine, cosine], 1),
        np.concatenate([sine, sine], 1),
        np.concatenate([cosine, np.ones_like(cosine)], 1),
        np.concatenate([sine, np.zeros_like(sine)], 1),
    )
    return tuple(jnp.asarray(table, F32) for table in tables)


def prefix(x, axis, combine, identity):
    count, here = (lax.axis_size(axis), lax.axis_index(axis))
    everything = jax.tree.map(lambda part: lax.all_gather(part, axis), x)
    start = jax.tree.map(
        lambda part, zero: jnp.broadcast_to(jnp.asarray(zero, part.dtype), part.shape), x, identity
    )

    def hop(k, before):
        reached = k < here
        new = combine(before, jax.tree.map(lambda part: part[k], everything))
        return jax.tree.map(lambda a, b: jnp.where(reached, a, b), new, before)

    return lax.fori_loop(0, count, hop, start)


def combine(earlier, later):
    return (earlier[0] * later[0], later[0] * earlier[1] + later[1])


def body(
    tokens,
    document_index,
    block_mask,
    slot_keys,
    mem_init,
    retain,
    attn_gain,
    mlp_gain,
    w_query,
    w_kv,
    w_out,
    w_gate_up,
    w_down,
):
    seg_local = document_index.shape[0] // SEG_LEN
    rows_all = seg_local * SEG_LEN
    cols_query = w_query.shape[2]
    local_heads = cols_query // HD
    group = HEADS // KV_HEADS
    local_kv = local_heads // group
    scale = HD ** (-0.5)
    tables = lane_tables()
    n = lax.axis_size("head")
    docs = document_index.reshape(seg_local, SEG_LEN)
    causal = jnp.arange(SEG_LEN)[:, None] >= jnp.arange(SEG_LEN)[None, :]
    rest = tokens
    query, pairs = gather_project(n, 0, 0, tokens, attn_gain[:1], w_query, w_kv, tables)
    stored = []
    for layer in range(DEPTH_NUMBER):
        pairs = pairs.reshape(rows_all, local_kv, 2, HD)
        lookup_vectors = pairs[:, :, 0]
        values = pairs[:, :, 1]
        query = query.reshape(seg_local, SEG_LEN, local_kv, group, HD)
        lookup_vectors = lookup_vectors.reshape(seg_local, SEG_LEN, local_kv, HD)
        values = values.reshape(seg_local, SEG_LEN, local_kv, HD)
        slots = slot_keys[layer].reshape(MEM, local_kv, group, HD)
        write_scores = (
            jnp.einsum(
                "mkgd,sjkd->skgmj", slots, lookup_vectors, preferred_element_type=jnp.float32
            )
            * scale
        )
        write_probs = jax.nn.softmax(write_scores, axis=-1).astype(jnp.bfloat16)
        written = jnp.einsum(
            "skgmj,sjkd->smkgd", write_probs, values, preferred_element_type=jnp.float32
        ).reshape(seg_local, MEM, cols_query)
        rates = jnp.repeat(retain[layer], HD, axis=1)[:, None, :]
        keep_total = jnp.ones((1, cols_query), jnp.float32)
        add_total = jnp.zeros((MEM, cols_query), jnp.float32)
        segment = 0
        keep_total = keep_total * rates[segment]
        add_total = rates[segment] * add_total + (1.0 - rates[segment]) * written[segment]
        identity = (
            jnp.ones((1, cols_query), jnp.float32),
            jnp.zeros((MEM, cols_query), jnp.float32),
        )
        keep_before, add_before = prefix((keep_total, add_total), "seg", combine, identity)
        state = keep_before * mem_init[layer] + add_before
        segment = 0
        memory_read = state.astype(jnp.bfloat16).reshape(MEM, local_kv, group, HD)
        state = rates[segment] * state + (1.0 - rates[segment]) * written[segment]
        after_list = [state]
        blocks = jnp.repeat(jnp.repeat(block_mask[segment], BLOCK, axis=0), BLOCK, axis=1)
        allowed = causal & (docs[segment][:, None] == docs[segment][None, :]) & (blocks == 1)
        slot_scores = (
            jnp.einsum("ikgd,mkgd->kgim", query[segment], slots, preferred_element_type=jnp.float32)
            * scale
        )
        token_scores = (
            jnp.einsum(
                "ikgd,jkd->kgij",
                query[segment],
                lookup_vectors[segment],
                preferred_element_type=jnp.float32,
            )
            * scale
        )
        token_scores = jnp.where(allowed, token_scores, -jnp.inf)
        probs = jax.nn.softmax(
            jnp.concatenate([slot_scores, token_scores], axis=-1), axis=-1
        ).astype(jnp.bfloat16)
        result = jnp.einsum(
            "kgim,mkgd->ikgd", probs[..., :MEM], memory_read, preferred_element_type=jnp.float32
        )
        result = result + jnp.einsum(
            "kgij,jkd->ikgd", probs[..., MEM:], values[segment], preferred_element_type=jnp.float32
        )
        outputs = result.reshape(SEG_LEN, cols_query).astype(jnp.bfloat16)
        stored.append(jnp.stack(after_list))
        widening = jnp.swapaxes(w_gate_up[layer], 0, 1)
        inner, rest = exchange(
            n, layer, 1 + 2 * layer, outputs, w_out, rest, mlp_gain[layer : layer + 1], (widening,)
        )
        if layer + 1 < DEPTH_NUMBER:
            query, pairs, rest = exchange(
                n, layer, 2 + 2 * layer, inner, w_down, rest, attn_gain[layer + 1 : layer + 2],
                (w_query, w_kv), tables,
            )
        else:
            stream = scatter(n, layer, 2 + 2 * layer, inner, w_down, rest)
    return (stream, jnp.stack(stored))


def solution(mesh):
    return jax.shard_map(
        body,
        mesh=mesh,
        in_specs=(
            P(("seg", "head"), None),
            P("seg"),
            P("seg", None, None),
            P(None, None, "head"),
            P(None, None, "head"),
            P(None, "seg", "head"),
            P(),
            P(),
            P(None, None, "head"),
            P(None, None, "head"),
            P(None, "head", None),
            P(None, None, None, "head"),
            P(None, "head", None),
        ),
        out_specs=(P(("seg", "head"), None), P(None, "seg", None, "head")),
        check_vma=False,
    )
```

```python
import functools

import jax
import jax.numpy as jnp
import numpy as np
from jax import lax
from jax.experimental import pallas as pl
from jax.experimental.pallas import tpu as pltpu
from jax.sharding import PartitionSpec as P

HEADS = 32
KV_HEADS = 8
HD = 64
MEM = 128
SEG_LEN = 512
BLOCK = 128
DEPTH_NUMBER = 2
CHUNK = 32
LAG = 2
MESH = pl.DeviceIdType.MESH
F32 = jnp.float32
BF16 = jnp.bfloat16


def enter(me, n):
    barrier = pltpu.get_barrier_semaphore()

    @pl.when(me > 0)
    def _():
        pl.semaphore_signal(barrier, inc=1, device_id={"head": me - 1}, device_id_type=MESH)

    @pl.when(me < n - 1)
    def _():
        pl.semaphore_signal(barrier, inc=1, device_id={"head": me + 1}, device_id_type=MESH)

    @pl.when((me > 0) & (me < n - 1))
    def _():
        pl.semaphore_wait(barrier, 2)

    @pl.when((me == 0) | (me == n - 1))
    def _():
        pl.semaphore_wait(barrier, 1)


def remote(source, target, send, recv, to):
    return pltpu.make_async_remote_copy(
        src_ref=source,
        dst_ref=target,
        send_sem=send,
        recv_sem=recv,
        device_id={"head": to},
        device_id_type=MESH,
    )


def normed_rows(value, gain):
    factor = lax.rsqrt(jnp.mean(value * value, axis=-1, keepdims=True) + 1e-05)
    return (value * factor * gain).astype(BF16)


def rope_lanes(value, cosine, sine):
    lane = lax.broadcasted_iota(jnp.int32, value.shape, 1)
    turned = jnp.where(lane % HD < HD // 2, pltpu.roll(value, 96, 1), pltpu.roll(value, 32, 1))
    return value * cosine + turned * sine


def project_rows(rows, x, wq, wkv, tables, q_out, kv_out):
    cosine, sine, cosine_kv, sine_kv = (table[rows, :] for table in tables)
    block = x[rows, :]
    query = jnp.dot(block, wq[...], preferred_element_type=F32)
    for at in range(0, query.shape[1], 128):
        q_out[rows, at : at + 128] = rope_lanes(query[:, at : at + 128], cosine, sine).astype(BF16)
    pairs = jnp.dot(block, wkv[...], preferred_element_type=F32)
    for at in range(0, pairs.shape[1], 128):
        kv_out[rows, at : at + 128] = rope_lanes(
            pairs[:, at : at + 128], cosine_kv, sine_kv
        ).astype(BF16)


def widen_rows(rows, x, w, out):
    block = x[rows, :]
    tile = 256

    def step(i, carry):
        cols = pl.ds(pl.multiple_of(i * tile, tile), tile)
        gate = jnp.dot(block, w[0, :, cols], preferred_element_type=F32)
        up = jnp.dot(block, w[1, :, cols], preferred_element_type=F32)
        out[rows, cols] = (gate / (1.0 + jnp.exp(-gate)) * up).astype(BF16)
        return carry

    lax.fori_loop(0, out.shape[1] // tile, step, 0)


def partial_rows(rows, x, w, part):
    block = x[rows, :]
    tile = 512

    def step(i, carry):
        cols = pl.ds(pl.multiple_of(i * tile, tile), tile)
        part[rows, cols] = jnp.dot(block, w[:, cols], preferred_element_type=F32)
        return carry

    lax.fori_loop(0, part.shape[1] // tile, step, 0)


def add_rest(me, n, part, rest):
    held = rest.shape[0]
    if held * n == part.shape[0]:
        rows = pl.ds(pl.multiple_of(me * held, held), held)
        part[rows, :] += rest[...]
    else:

        @pl.when(me == 0)
        def _():
            part[:held, :] += rest[...]

        @pl.when(me == n - 1)
        def _():
            part[held:, :] += rest[...]


def gather_kernel(n, layer, tokens, gain, wq_hbm, wkv_hbm, cos_q, sin_q, cos_kv, sin_kv,
                  q_out, kv_out, x, wq, wkv, load, send, recv):
    me = lax.axis_index("head")
    loads = [
        pltpu.make_async_copy(wq_hbm.at[layer], wq, load.at[0]),
        pltpu.make_async_copy(wkv_hbm.at[layer], wkv, load.at[1]),
    ]
    for copy in loads:
        copy.start()
    mine = tokens.shape[0]
    pieces = mine // CHUNK
    enter(me, n)

    def hop(way, shard, piece):
        rows = pl.ds(pl.multiple_of(shard * mine + piece * CHUNK, CHUNK), CHUNK)
        to = me + 1 if way == 0 else me - 1
        to = jnp.clip(to, 0, n - 1)
        at = shard * pieces + piece
        return remote(x.at[rows], x.at[rows], send.at[way, at], recv.at[way, at], to)

    for piece in range(pieces):
        rows = pl.ds(pl.multiple_of(me * mine + piece * CHUNK, CHUNK), CHUNK)
        x[rows, :] = normed_rows(tokens[piece * CHUNK : (piece + 1) * CHUNK, :], gain[...])

        @pl.when(me < n - 1)
        def _():
            hop(0, me, piece).start()

        @pl.when(me > 0)
        def _():
            hop(1, me, piece).start()

    for copy in loads:
        copy.wait()
    tables = (cos_q, sin_q, cos_kv, sin_kv)

    def project(shard):
        rows = pl.ds(pl.multiple_of(shard * mine, mine), mine)
        project_rows(rows, x, wq, wkv, tables, q_out, kv_out)

    project(me)
    for far in range(1, n):
        for piece in range(pieces):

            @pl.when(me - far >= 0)
            def _():
                hop(0, me - far, piece).wait_recv()

                @pl.when(me < n - 1)
                def _():
                    hop(0, me - far, piece).start()

            @pl.when(me + far < n)
            def _():
                hop(1, me + far, piece).wait_recv()

                @pl.when(me > 0)
                def _():
                    hop(1, me + far, piece).start()

        @pl.when(me - far >= 0)
        def _():
            project(me - far)

        @pl.when(me + far < n)
        def _():
            project(me + far)

    for shard in range(n):
        for piece in range(pieces):

            @pl.when((shard <= me) & (me < n - 1))
            def _():
                hop(0, shard, piece).wait_send()

            @pl.when((shard >= me) & (me > 0))
            def _():
                hop(1, shard, piece).wait_send()


def exchange_kernel(n, layer, wide, *refs):
    me = lax.axis_index("head")
    if wide:
        (x, w_hbm, rest, gain, after_hbm, out, stream,
         part, outgoing, arriving, gathered, w, after, load,
         sum_send, sum_recv, all_send, all_recv) = refs
        loads = [
            pltpu.make_async_copy(w_hbm.at[layer], w, load.at[0]),
            pltpu.make_async_copy(after_hbm, after, load.at[1]),
        ]
    else:
        (x, w_hbm, rest, gain, wq_hbm, wkv_hbm, cos_q, sin_q, cos_kv, sin_kv, q_out, kv_out, stream,
         part, outgoing, arriving, gathered, w, wq, wkv, load,
         sum_send, sum_recv, all_send, all_recv) = refs
        loads = [
            pltpu.make_async_copy(w_hbm.at[layer], w, load.at[0]),
            pltpu.make_async_copy(wq_hbm.at[layer + 1], wq, load.at[1]),
            pltpu.make_async_copy(wkv_hbm.at[layer + 1], wkv, load.at[2]),
        ]
    for copy in loads:
        copy.start()
    half = part.shape[0] // 2
    count = half // CHUNK
    enter(me, n)
    loads[0].wait()
    for block in range(0, half, BLOCK):
        for way in (0, 1):
            partial_rows(pl.ds(way * half + block, BLOCK), x, w, part)
    add_rest(me, n, part, rest)

    def place(way, t):
        return pl.ds(pl.multiple_of(way * half + t * CHUNK, CHUNK), CHUNK)

    def sum_hop(way, t):
        rows = place(way, t)
        to = jnp.clip(me - 1 if way == 0 else me + 1, 0, n - 1)
        return remote(outgoing.at[rows], arriving.at[rows], sum_send.at[way, t],
                      sum_recv.at[way, t], to)

    def all_hop(way, t):
        rows = place(way, t)
        to = jnp.clip(me + 1 if way == 0 else me - 1, 0, n - 1)
        return remote(gathered.at[rows], gathered.at[rows], all_send.at[way, t],
                      all_recv.at[way, t], to)

    ends = ((n - 1, 0), (0, n - 1))

    def add_up(way, t):
        first, owner = ends[way]
        rows = place(way, t)

        @pl.when(me == first)
        def _():
            outgoing[rows, :] = part[rows, :].astype(BF16)
            sum_hop(way, t).start()

        @pl.when((me != first) & (me != owner))
        def _():
            sum_hop(way, t).wait_recv()
            outgoing[rows, :] = (part[rows, :] + arriving[rows, :].astype(F32)).astype(BF16)
            sum_hop(way, t).start()

        @pl.when(me == owner)
        def _():
            sum_hop(way, t).wait_recv()
            total = part[rows, :] + arriving[rows, :].astype(F32)
            stream[pl.ds(pl.multiple_of(t * CHUNK, CHUNK), CHUNK), :] = total
            gathered[rows, :] = normed_rows(total, gain[...])
            all_hop(way, t).start()

    def hand_on(way, t):
        first, owner = ends[way]

        @pl.when(me != owner)
        def _():
            all_hop(way, t).wait_recv()

            @pl.when(me != first)
            def _():
                all_hop(way, t).start()

    def finish(way, block):
        rows = pl.ds(pl.multiple_of(way * half + block * BLOCK, BLOCK), BLOCK)
        if wide:
            widen_rows(rows, gathered, after, out)
        else:
            project_rows(rows, gathered, wq, wkv, (cos_q, sin_q, cos_kv, sin_kv), q_out, kv_out)

    per = BLOCK // CHUNK

    def tick(now, carry):
        down, back = [], []
        for way in (0, 1):
            far = n - 1 - me if way == 0 else me
            down.append(now - LAG * far)
            back.append(now - LAG * (n - 1) - LAG * (n - 1 - far))
        for way in (0, 1):

            @pl.when((down[way] >= 0) & (down[way] < count))
            def _():
                add_up(way, down[way])

        for way in (0, 1):

            @pl.when((back[way] >= 0) & (back[way] < count))
            def _():
                hand_on(way, back[way])

        @pl.when(now == LAG * (n - 1))
        def _():
            for copy in loads[1:]:
                copy.wait()

        for way in (0, 1):

            @pl.when((back[way] >= 0) & (back[way] < count) & (back[way] % per == per - 1))
            def _():
                finish(way, back[way] // per)

        return carry

    lax.fori_loop(0, 2 * LAG * (n - 1) + count, tick, 0)

    def drain(t, carry):
        for way in (0, 1):
            first, owner = ends[way]

            @pl.when(me != owner)
            def _():
                sum_hop(way, t).wait_send()

            @pl.when(me != first)
            def _():
                all_hop(way, t).wait_send()

        return carry

    lax.fori_loop(0, count, drain, 0)


def scatter_kernel(n, layer, x, w_hbm, rest, out, part, outgoing, arriving, w, load, send, recv):
    me = lax.axis_index("head")
    copy = pltpu.make_async_copy(w_hbm.at[layer], w, load.at[0])
    copy.start()
    mine = out.shape[0]
    pieces = mine // CHUNK
    enter(me, n)
    copy.wait()
    for shard in range(n):
        partial_rows(pl.ds(shard * mine, mine), x, w, part)
    add_rest(me, n, part, rest)

    def place(at):
        return pl.ds(pl.multiple_of(at * CHUNK, CHUNK), CHUNK)

    def hop(way, at):
        rows = place(at)
        to = jnp.clip(me + 1 if way == 0 else me - 1, 0, n - 1)
        return remote(outgoing.at[way, rows], arriving.at[way, rows], send.at[way, at],
                      recv.at[way, at], to)

    def step(i, carry):
        for way in (0, 1):
            shard = n - 1 - i // pieces if way == 0 else i // pieces
            at = shard * pieces + i % pieces
            rows = place(at)
            ahead = me < shard if way == 0 else me > shard
            edge = me == 0 if way == 0 else me == n - 1

            @pl.when(ahead & edge)
            def _():
                outgoing[way, rows, :] = part[rows, :].astype(BF16)
                hop(way, at).start()

            @pl.when(ahead & jnp.logical_not(edge))
            def _():
                hop(way, at).wait_recv()
                outgoing[way, rows, :] = (
                    part[rows, :] + arriving[way, rows, :].astype(F32)
                ).astype(BF16)
                hop(way, at).start()

        return carry

    lax.fori_loop(0, (n - 1) * pieces, step, 0)
    for piece in range(pieces):
        at = me * pieces + piece
        here = slice(piece * CHUNK, (piece + 1) * CHUNK)
        out[here, :] = part[place(at), :]

        @pl.when(me > 0)
        def _():
            hop(0, at).wait_recv()
            out[here, :] += arriving[0, place(at), :].astype(F32)

        @pl.when(me < n - 1)
        def _():
            hop(1, at).wait_recv()
            out[here, :] += arriving[1, place(at), :].astype(F32)

    def drain(at, carry):
        shard = at // pieces

        @pl.when(me < shard)
        def _():
            hop(0, at).wait_send()

        @pl.when(me > shard)
        def _():
            hop(1, at).wait_send()

        return carry

    lax.fori_loop(0, n * pieces, drain, 0)


VM = pl.BlockSpec(memory_space=pltpu.VMEM)
HB = pl.BlockSpec(memory_space=pl.ANY)


def parameters(number):
    return pltpu.CompilerParams(
        collective_id=number, has_side_effects=True, vmem_limit_bytes=48 * 1024 * 1024
    )


def dma(*shape):
    return pltpu.SemaphoreType.DMA(shape)


def gather_project(n, layer, number, tokens, gain, wq, wkv, tables):
    mine, width = tokens.shape
    rows, cq, ck = mine * n, wq.shape[2], wkv.shape[2]
    return pl.pallas_call(
        functools.partial(gather_kernel, n, layer),
        out_shape=[jax.ShapeDtypeStruct((rows, cq), BF16), jax.ShapeDtypeStruct((rows, ck), BF16)],
        in_specs=[VM, VM, HB, HB] + [VM] * 4,
        out_specs=[VM, VM],
        scratch_shapes=[
            pltpu.VMEM((rows, width), BF16),
            pltpu.VMEM(wq.shape[1:], BF16),
            pltpu.VMEM(wkv.shape[1:], BF16),
            dma(2),
            dma(2, rows // CHUNK),
            dma(2, rows // CHUNK),
        ],
        compiler_params=parameters(number),
        name="gather_project",
    )(tokens, gain, wq, wkv, *tables)


def exchange(n, layer, number, x, w, rest, gain, after, tables=None):
    rows, width = x.shape[0], w.shape[2]
    half = rows // 2
    wide = tables is None
    count = half // CHUNK
    if wide:
        outs = [jax.ShapeDtypeStruct((rows, after[0].shape[2]), BF16)]
        kept = [pltpu.VMEM(after[0].shape, BF16)]
    else:
        outs = [jax.ShapeDtypeStruct((rows, part.shape[2]), BF16) for part in after]
        kept = [pltpu.VMEM(part.shape[1:], BF16) for part in after]
    outs.append(jax.ShapeDtypeStruct((half, width), F32))
    more = () if wide else tables
    return pl.pallas_call(
        functools.partial(exchange_kernel, n, layer, wide),
        out_shape=outs,
        in_specs=[VM, HB, VM, VM] + [HB] * len(after) + [VM] * len(more),
        out_specs=[VM] * len(outs),
        scratch_shapes=[
            pltpu.VMEM((rows, width), F32),
            pltpu.VMEM((rows, width), BF16),
            pltpu.VMEM((rows, width), BF16),
            pltpu.VMEM((rows, width), BF16),
            pltpu.VMEM(w.shape[1:], BF16),
            *kept,
            dma(3),
            dma(2, count),
            dma(2, count),
            dma(2, count),
            dma(2, count),
        ],
        compiler_params=parameters(number),
        name="exchange",
    )(x, w, rest, gain, *after, *more)


def scatter(n, layer, number, x, w, rest):
    rows, width = x.shape[0], w.shape[2]
    return pl.pallas_call(
        functools.partial(scatter_kernel, n, layer),
        out_shape=jax.ShapeDtypeStruct((rows // n, width), F32),
        in_specs=[VM, HB, VM],
        out_specs=VM,
        scratch_shapes=[
            pltpu.VMEM((rows, width), F32),
            pltpu.VMEM((2, rows, width), BF16),
            pltpu.VMEM((2, rows, width), BF16),
            pltpu.VMEM(w.shape[1:], BF16),
            dma(1),
            dma(2, rows // CHUNK),
            dma(2, rows // CHUNK),
        ],
        compiler_params=parameters(number),
        name="scatter",
    )(x, w, rest)


def lane_tables():
    freq = 500000.0 ** (-(np.arange(HD // 2) * 2.0 / HD))
    angle = np.arange(SEG_LEN)[:, None] * freq[None, :]
    c, s = np.cos(angle), np.sin(angle)
    cosine, sine = np.concatenate([c, c], 1), np.concatenate([-s, s], 1)
    tables = (
        np.concatenate([cosine, cosine], 1),
        np.concatenate([sine, sine], 1),
        np.concatenate([cosine, np.ones_like(cosine)], 1),
        np.concatenate([sine, np.zeros_like(sine)], 1),
    )
    return tuple(jnp.asarray(table, F32) for table in tables)


def heads_dot(a, b):
    return lax.dot_general(a, b, (((1,), (1,)), ((), ())), preferred_element_type=F32)


def attend_kernel(count, query, pairs, slots, bias, initial, weight, keep, rate, out, after,
                  written, box, probs, state, send, recv):
    me = lax.axis_index("seg")
    group = HEADS // KV_HEADS
    local_kv = pairs.shape[1] // (2 * HD)
    span = group * HD
    scale = HD ** (-0.5)
    barrier = pltpu.get_barrier_semaphore()

    def greet(k, carry):
        @pl.when(k != me)
        def _():
            pl.semaphore_signal(barrier, inc=1, device_id={"seg": k}, device_id_type=MESH)

        return carry

    lax.fori_loop(0, count, greet, 0)

    for g in range(local_kv):
        keys = pairs[:, 2 * g * HD : (2 * g + 1) * HD]
        values = pairs[:, (2 * g + 1) * HD : (2 * g + 2) * HD]
        stacked = jnp.concatenate(
            [slots[:, g * span + h * HD : g * span + (h + 1) * HD] for h in range(group)], axis=0
        )
        scores = heads_dot(stacked, keys) * scale
        top = jnp.exp(scores - jnp.max(scores, axis=-1, keepdims=True))
        share = (top / jnp.sum(top, axis=-1, keepdims=True)).astype(BF16)
        fresh = jnp.dot(share, values, preferred_element_type=F32)
        written[:, g * span : (g + 1) * span] = jnp.concatenate(
            [fresh[h * MEM : (h + 1) * MEM] for h in range(group)], axis=1
        )
    box[me] = written[...].astype(BF16)
    pl.semaphore_wait(barrier, count - 1)

    def hop(source, target):
        return pltpu.make_async_remote_copy(
            src_ref=box.at[source],
            dst_ref=box.at[source],
            send_sem=send.at[target],
            recv_sem=recv.at[source],
            device_id={"seg": target},
            device_id_type=MESH,
        )

    def post(k, carry):
        @pl.when(k > me)
        def _():
            hop(me, k).start()

        return carry

    lax.fori_loop(0, count, post, 0)
    blocks = query.shape[0] // BLOCK
    for g in range(local_kv):
        for b in range(blocks):
            rows, reach = slice(b * BLOCK, (b + 1) * BLOCK), (b + 1) * BLOCK
            parts = [
                query[rows, g * span + h * HD : g * span + (h + 1) * HD] for h in range(group)
            ]
            slot_scores = jnp.concatenate(
                [
                    heads_dot(parts[h], slots[:, g * span + h * HD : g * span + (h + 1) * HD])
                    for h in range(group)
                ],
                axis=0,
            ) * scale
            shade = bias[rows, :reach]
            token_scores = heads_dot(
                jnp.concatenate(parts, axis=0), pairs[:reach, 2 * g * HD : (2 * g + 1) * HD]
            ) * scale + jnp.concatenate([shade] * group, axis=0)
            peak = jnp.maximum(
                jnp.max(slot_scores, axis=-1, keepdims=True),
                jnp.max(token_scores, axis=-1, keepdims=True),
            )
            slot_top = jnp.exp(slot_scores - peak)
            token_top = jnp.exp(token_scores - peak)
            total = jnp.sum(slot_top, axis=-1, keepdims=True) + jnp.sum(
                token_top, axis=-1, keepdims=True
            )
            inverse = 1.0 / total
            probs[g, b, :, :MEM] = (slot_top * inverse).astype(BF16)
            probs[g, b, :, MEM : MEM + reach] = (token_top * inverse).astype(BF16)
    state[...] = keep[...] * initial[...]

    def take(k, carry):
        @pl.when(k < me)
        def _():
            hop(k, me).wait_recv()
            state[...] += weight[k] * box[k].astype(F32)

        return carry

    lax.fori_loop(0, count, take, 0)
    after[...] = rate[...] * state[...] + (1.0 - rate[...]) * written[...]
    for g in range(local_kv):
        memory = state[:, g * span : (g + 1) * span].astype(BF16)
        for b in range(blocks):
            reach = (b + 1) * BLOCK
            found = jnp.dot(
                probs[g, b, :, MEM : MEM + reach],
                pairs[:reach, (2 * g + 1) * HD : (2 * g + 2) * HD],
                preferred_element_type=F32,
            )
            pieces = [
                found[h * BLOCK : (h + 1) * BLOCK]
                + jnp.dot(
                    probs[g, b, h * BLOCK : (h + 1) * BLOCK, :MEM],
                    memory[:, h * HD : (h + 1) * HD],
                    preferred_element_type=F32,
                )
                for h in range(group)
            ]
            out[b * BLOCK : (b + 1) * BLOCK, g * span : (g + 1) * span] = jnp.concatenate(
                pieces, axis=1
            ).astype(BF16)

    def drain(k, carry):
        @pl.when(k > me)
        def _():
            hop(me, k).wait_send()

        return carry

    lax.fori_loop(0, count, drain, 0)


def attend(count, number, query, pairs, slots, bias, initial, weight, keep, rate):
    rows, columns = query.shape
    local_kv = pairs.shape[1] // (2 * HD)
    group = HEADS // KV_HEADS
    return pl.pallas_call(
        functools.partial(attend_kernel, count),
        out_shape=[
            jax.ShapeDtypeStruct((rows, columns), BF16),
            jax.ShapeDtypeStruct((MEM, columns), F32),
        ],
        in_specs=[VM] * 8,
        out_specs=[VM, VM],
        scratch_shapes=[
            pltpu.VMEM((MEM, columns), F32),
            pltpu.VMEM((count, MEM, columns), BF16),
            pltpu.VMEM((local_kv, rows // BLOCK, group * BLOCK, MEM + rows), BF16),
            pltpu.VMEM((MEM, columns), F32),
            dma(count),
            dma(count),
        ],
        compiler_params=parameters(number),
        name="attend",
    )(query, pairs, slots, bias, initial, weight, keep, rate)


def carry_weights(retain):
    count, here = lax.axis_size("seg"), lax.axis_index("seg")
    rates = lax.all_gather(retain[:, 0], "seg")
    at = jnp.arange(count)
    between = (at[None, :] > at[:, None]) & (at[None, :] < here)
    keep = jnp.prod(jnp.where(between[:, :, None, None], rates[None], 1.0), axis=1)
    weight = jnp.where((at < here)[:, None, None], (1.0 - rates) * keep, 0.0)
    whole = jnp.prod(jnp.where((at < here)[:, None, None], rates, 1.0), axis=0)
    weight = jnp.repeat(weight.transpose(1, 0, 2), HD, axis=2)[:, :, None, :]
    return weight, jnp.repeat(whole, HD, axis=1)[:, None, :], jnp.repeat(retain, HD, axis=2)


def body(
    tokens,
    document_index,
    block_mask,
    slot_keys,
    mem_init,
    retain,
    attn_gain,
    mlp_gain,
    w_query,
    w_kv,
    w_out,
    w_gate_up,
    w_down,
):
    n, count = lax.axis_size("head"), lax.axis_size("seg")
    tables = lane_tables()
    weight, keep, rate = carry_weights(retain)
    causal = jnp.arange(SEG_LEN)[:, None] >= jnp.arange(SEG_LEN)[None, :]
    blocks = jnp.repeat(jnp.repeat(block_mask[0], BLOCK, axis=0), BLOCK, axis=1)
    same = document_index[:, None] == document_index[None, :]
    bias = jnp.where(causal & same & (blocks == 1), 0.0, -jnp.inf).astype(F32)
    query, pairs = gather_project(n, 0, 0, tokens, attn_gain[:1], w_query, w_kv, tables)
    rest = tokens
    stored = []
    for layer in range(DEPTH_NUMBER):
        attended, after = attend(
            count, 5 + layer, query, pairs, slot_keys[layer], bias, mem_init[layer],
            weight[layer], keep[layer], rate[layer],
        )
        stored.append(after)
        widening = jnp.swapaxes(w_gate_up[layer], 0, 1)
        inner, rest = exchange(
            n, layer, 1 + 2 * layer, attended, w_out, rest, mlp_gain[layer : layer + 1], (widening,)
        )
        if layer + 1 < DEPTH_NUMBER:
            query, pairs, rest = exchange(
                n, layer, 2 + 2 * layer, inner, w_down, rest, attn_gain[layer + 1 : layer + 2],
                (w_query, w_kv), tables,
            )
        else:
            stream = scatter(n, layer, 2 + 2 * layer, inner, w_down, rest)
    return (stream, jnp.stack(stored)[:, None])


def solution(mesh):
    return jax.shard_map(
        body,
        mesh=mesh,
        in_specs=(
            P(("seg", "head"), None),
            P("seg"),
            P("seg", None, None),
            P(None, None, "head"),
            P(None, None, "head"),
            P(None, "seg", "head"),
            P(),
            P(),
            P(None, None, "head"),
            P(None, None, "head"),
            P(None, "head", None),
            P(None, None, None, "head"),
            P(None, "head", None),
        ),
        out_specs=(P(("seg", "head"), None), P(None, "seg", None, "head")),
        check_vma=False,
    )
```

```python
import functools

import jax
import jax.numpy as jnp
import numpy as np
from jax import lax
from jax.experimental import pallas as pl
from jax.experimental.pallas import tpu as pltpu
from jax.sharding import PartitionSpec as P

HEADS = 32
KV_HEADS = 8
HD = 64
MEM = 128
SEG_LEN = 512
BLOCK = 128
DEPTH_NUMBER = 2
CHUNK = 16
PIECE = 32
LAG = 2
MESH = pl.DeviceIdType.MESH
F32 = jnp.float32
BF16 = jnp.bfloat16


def enter(me, n):
    barrier = pltpu.get_barrier_semaphore()

    @pl.when(me > 0)
    def _():
        pl.semaphore_signal(barrier, inc=1, device_id={"head": me - 1}, device_id_type=MESH)

    @pl.when(me < n - 1)
    def _():
        pl.semaphore_signal(barrier, inc=1, device_id={"head": me + 1}, device_id_type=MESH)

    @pl.when((me > 0) & (me < n - 1))
    def _():
        pl.semaphore_wait(barrier, 2)

    @pl.when((me == 0) | (me == n - 1))
    def _():
        pl.semaphore_wait(barrier, 1)


def remote(source, target, send, recv, to):
    return pltpu.make_async_remote_copy(
        src_ref=source,
        dst_ref=target,
        send_sem=send,
        recv_sem=recv,
        device_id={"head": to},
        device_id_type=MESH,
    )


def normed_rows(value, gain):
    factor = lax.rsqrt(jnp.mean(value * value, axis=-1, keepdims=True) + 1e-05)
    return (value * factor * gain).astype(BF16)


def rope_lanes(value, cosine, sine):
    lane = lax.broadcasted_iota(jnp.int32, value.shape, 1)
    turned = jnp.where(lane % HD < HD // 2, pltpu.roll(value, 96, 1), pltpu.roll(value, 32, 1))
    return value * cosine + turned * sine


def project_rows(rows, x, wq, wkv, tables, q_out, kv_out):
    cosine, sine, cosine_kv, sine_kv = (table[rows, :] for table in tables)
    block = x[rows, :]
    query = jnp.dot(block, wq[...], preferred_element_type=F32)
    for at in range(0, query.shape[1], 128):
        q_out[rows, at : at + 128] = rope_lanes(query[:, at : at + 128], cosine, sine).astype(BF16)
    pairs = jnp.dot(block, wkv[...], preferred_element_type=F32)
    for at in range(0, pairs.shape[1], 128):
        kv_out[rows, at : at + 128] = rope_lanes(
            pairs[:, at : at + 128], cosine_kv, sine_kv
        ).astype(BF16)


def widen_rows(rows, x, w, out):
    block = x[rows, :]
    tile = 256

    def step(i, carry):
        cols = pl.ds(pl.multiple_of(i * tile, tile), tile)
        gate = jnp.dot(block, w[0, :, cols], preferred_element_type=F32)
        up = jnp.dot(block, w[1, :, cols], preferred_element_type=F32)
        out[rows, cols] = (gate / (1.0 + jnp.exp(-gate)) * up).astype(BF16)
        return carry

    lax.fori_loop(0, out.shape[1] // tile, step, 0)


def partial_rows(rows, x, w, part):
    block = x[rows, :]
    tile = 512

    def step(i, carry):
        cols = pl.ds(pl.multiple_of(i * tile, tile), tile)
        part[rows, cols] = jnp.dot(block, w[:, cols], preferred_element_type=F32)
        return carry

    lax.fori_loop(0, part.shape[1] // tile, step, 0)


def add_rest(me, n, part, rest):
    held = rest.shape[0]
    if held * n == part.shape[0]:
        rows = pl.ds(pl.multiple_of(me * held, held), held)
        part[rows, :] += rest[...]
    else:

        @pl.when(me == 0)
        def _():
            part[:held, :] += rest[...]

        @pl.when(me == n - 1)
        def _():
            part[held:, :] += rest[...]


def gather_kernel(n, layer, tokens, gain, wq_hbm, wkv_hbm, cos_q, sin_q, cos_kv, sin_kv,
                  q_out, kv_out, x, wq, wkv, load, send, recv):
    me = lax.axis_index("head")
    loads = [
        pltpu.make_async_copy(wq_hbm.at[layer], wq, load.at[0]),
        pltpu.make_async_copy(wkv_hbm.at[layer], wkv, load.at[1]),
    ]
    for copy in loads:
        copy.start()
    mine = tokens.shape[0]
    pieces = mine // PIECE
    enter(me, n)

    def hop(way, shard, piece):
        rows = pl.ds(pl.multiple_of(shard * mine + piece * PIECE, PIECE), PIECE)
        to = me + 1 if way == 0 else me - 1
        to = jnp.clip(to, 0, n - 1)
        at = shard * pieces + piece
        return remote(x.at[rows], x.at[rows], send.at[way, at], recv.at[way, at], to)

    for piece in range(pieces):
        rows = pl.ds(pl.multiple_of(me * mine + piece * PIECE, PIECE), PIECE)
        x[rows, :] = normed_rows(tokens[piece * PIECE : (piece + 1) * PIECE, :], gain[...])

        @pl.when(me < n - 1)
        def _():
            hop(0, me, piece).start()

        @pl.when(me > 0)
        def _():
            hop(1, me, piece).start()

    for copy in loads:
        copy.wait()
    tables = (cos_q, sin_q, cos_kv, sin_kv)

    def project(shard):
        rows = pl.ds(pl.multiple_of(shard * mine, mine), mine)
        project_rows(rows, x, wq, wkv, tables, q_out, kv_out)

    project(me)
    for far in range(1, n):
        for piece in range(pieces):

            @pl.when(me - far >= 0)
            def _():
                hop(0, me - far, piece).wait_recv()

                @pl.when(me < n - 1)
                def _():
                    hop(0, me - far, piece).start()

            @pl.when(me + far < n)
            def _():
                hop(1, me + far, piece).wait_recv()

                @pl.when(me > 0)
                def _():
                    hop(1, me + far, piece).start()

        @pl.when(me - far >= 0)
        def _():
            project(me - far)

        @pl.when(me + far < n)
        def _():
            project(me + far)

    for shard in range(n):
        for piece in range(pieces):

            @pl.when((shard <= me) & (me < n - 1))
            def _():
                hop(0, shard, piece).wait_send()

            @pl.when((shard >= me) & (me > 0))
            def _():
                hop(1, shard, piece).wait_send()


def exchange_kernel(n, layer, wide, *refs):
    me = lax.axis_index("head")
    if wide:
        (x, w_hbm, rest, gain, after_hbm, out, stream,
         part, outgoing, arriving, gathered, w, after, load,
         sum_send, sum_recv, all_send, all_recv) = refs
        loads = [
            pltpu.make_async_copy(w_hbm.at[layer], w, load.at[0]),
            pltpu.make_async_copy(after_hbm, after, load.at[1]),
        ]
    else:
        (x, w_hbm, rest, gain, wq_hbm, wkv_hbm, cos_q, sin_q, cos_kv, sin_kv, q_out, kv_out, stream,
         part, outgoing, arriving, gathered, w, wq, wkv, load,
         sum_send, sum_recv, all_send, all_recv) = refs
        loads = [
            pltpu.make_async_copy(w_hbm.at[layer], w, load.at[0]),
            pltpu.make_async_copy(wq_hbm.at[layer + 1], wq, load.at[1]),
            pltpu.make_async_copy(wkv_hbm.at[layer + 1], wkv, load.at[2]),
        ]
    for copy in loads:
        copy.start()
    half = part.shape[0] // 2
    count = half // CHUNK
    enter(me, n)
    loads[0].wait()
    for way in (0, 1):
        partial_rows(pl.ds(way * half, BLOCK), x, w, part)

    def place(way, t):
        return pl.ds(pl.multiple_of(way * half + t * CHUNK, CHUNK), CHUNK)

    def sum_hop(way, t):
        rows = place(way, t)
        to = jnp.clip(me - 1 if way == 0 else me + 1, 0, n - 1)
        return remote(outgoing.at[rows], arriving.at[rows], sum_send.at[way, t],
                      sum_recv.at[way, t], to)

    def all_hop(way, t):
        rows = place(way, t)
        to = jnp.clip(me + 1 if way == 0 else me - 1, 0, n - 1)
        return remote(gathered.at[rows], gathered.at[rows], all_send.at[way, t],
                      all_recv.at[way, t], to)

    ends = ((n - 1, 0), (0, n - 1))

    def add_up(way, t):
        first, owner = ends[way]
        rows = place(way, t)

        @pl.when(me == first)
        def _():
            outgoing[rows, :] = part[rows, :].astype(BF16)
            sum_hop(way, t).start()

        @pl.when((me != first) & (me != owner))
        def _():
            sum_hop(way, t).wait_recv()
            outgoing[rows, :] = (part[rows, :] + arriving[rows, :].astype(F32)).astype(BF16)
            sum_hop(way, t).start()

        @pl.when(me == owner)
        def _():
            sum_hop(way, t).wait_recv()
            total = part[rows, :] + arriving[rows, :].astype(F32)
            stream[pl.ds(pl.multiple_of(t * CHUNK, CHUNK), CHUNK), :] = total
            gathered[rows, :] = normed_rows(total, gain[...])
            all_hop(way, t).start()

    def hand_on(way, t):
        first, owner = ends[way]

        @pl.when(me != owner)
        def _():
            all_hop(way, t).wait_recv()

            @pl.when(me != first)
            def _():
                all_hop(way, t).start()

    def finish(way, block):
        rows = pl.ds(pl.multiple_of(way * half + block * BLOCK, BLOCK), BLOCK)
        if wide:
            widen_rows(rows, gathered, after, out)
        else:
            project_rows(rows, gathered, wq, wkv, (cos_q, sin_q, cos_kv, sin_kv), q_out, kv_out)

    per = BLOCK // CHUNK

    def tick(now, carry):
        down, back = [], []
        for way in (0, 1):
            far = n - 1 - me if way == 0 else me
            down.append(now - LAG * far)
            back.append(now - LAG * (n - 1) - LAG * (n - 1 - far))
        @pl.when(now == LAG)
        def _():
            for way in (0, 1):
                for block in range(BLOCK, half, BLOCK):
                    partial_rows(pl.ds(way * half + block, BLOCK), x, w, part)
            add_rest(me, n, part, rest)

        for way in (0, 1):

            @pl.when((down[way] >= 0) & (down[way] < count))
            def _():
                add_up(way, down[way])

        for way in (0, 1):

            @pl.when((back[way] >= 0) & (back[way] < count))
            def _():
                hand_on(way, back[way])

        @pl.when(now == LAG * (n - 1))
        def _():
            for copy in loads[1:]:
                copy.wait()

        for way in (0, 1):

            @pl.when((back[way] >= 0) & (back[way] < count) & (back[way] % per == per - 1))
            def _():
                finish(way, back[way] // per)

        return carry

    lax.fori_loop(0, 2 * LAG * (n - 1) + count, tick, 0)

    def drain(t, carry):
        for way in (0, 1):
            first, owner = ends[way]

            @pl.when(me != owner)
            def _():
                sum_hop(way, t).wait_send()

            @pl.when(me != first)
            def _():
                all_hop(way, t).wait_send()

        return carry

    lax.fori_loop(0, count, drain, 0)


def scatter_kernel(n, layer, x, w_hbm, rest, out, part, outgoing, arriving, w, load, send, recv):
    me = lax.axis_index("head")
    copy = pltpu.make_async_copy(w_hbm.at[layer], w, load.at[0])
    copy.start()
    mine = out.shape[0]
    pieces = mine // CHUNK
    enter(me, n)
    copy.wait()
    for shard in range(n):
        partial_rows(pl.ds(shard * mine, mine), x, w, part)
    add_rest(me, n, part, rest)

    def place(at):
        return pl.ds(pl.multiple_of(at * CHUNK, CHUNK), CHUNK)

    def hop(way, at):
        rows = place(at)
        to = jnp.clip(me + 1 if way == 0 else me - 1, 0, n - 1)
        return remote(outgoing.at[way, rows], arriving.at[way, rows], send.at[way, at],
                      recv.at[way, at], to)

    hops = (n - 1) * pieces

    def step(now, carry):
        for way in (0, 1):
            i = now - LAG * (me if way == 0 else n - 1 - me)
            valid = (i >= 0) & (i < hops)
            i = jnp.clip(i, 0, hops - 1)
            shard = n - 1 - i // pieces if way == 0 else i // pieces
            at = shard * pieces + i % pieces
            rows = place(at)
            ahead = valid & ((me < shard) if way == 0 else (me > shard))
            edge = me == 0 if way == 0 else me == n - 1

            @pl.when(ahead & edge)
            def _():
                outgoing[way, rows, :] = part[rows, :].astype(BF16)
                hop(way, at).start()

            @pl.when(ahead & jnp.logical_not(edge))
            def _():
                hop(way, at).wait_recv()
                outgoing[way, rows, :] = (
                    part[rows, :] + arriving[way, rows, :].astype(F32)
                ).astype(BF16)
                hop(way, at).start()

        return carry

    lax.fori_loop(0, hops + LAG * (n - 1), step, 0)
    for piece in range(pieces):
        at = me * pieces + piece
        here = slice(piece * CHUNK, (piece + 1) * CHUNK)
        out[here, :] = part[place(at), :]

        @pl.when(me > 0)
        def _():
            hop(0, at).wait_recv()
            out[here, :] += arriving[0, place(at), :].astype(F32)

        @pl.when(me < n - 1)
        def _():
            hop(1, at).wait_recv()
            out[here, :] += arriving[1, place(at), :].astype(F32)

    def drain(at, carry):
        shard = at // pieces

        @pl.when(me < shard)
        def _():
            hop(0, at).wait_send()

        @pl.when(me > shard)
        def _():
            hop(1, at).wait_send()

        return carry

    lax.fori_loop(0, n * pieces, drain, 0)


VM = pl.BlockSpec(memory_space=pltpu.VMEM)
HB = pl.BlockSpec(memory_space=pl.ANY)


def parameters(number):
    return pltpu.CompilerParams(
        collective_id=number, has_side_effects=True, vmem_limit_bytes=48 * 1024 * 1024
    )


def dma(*shape):
    return pltpu.SemaphoreType.DMA(shape)


def gather_project(n, layer, number, tokens, gain, wq, wkv, tables):
    mine, width = tokens.shape
    rows, cq, ck = mine * n, wq.shape[2], wkv.shape[2]
    return pl.pallas_call(
        functools.partial(gather_kernel, n, layer),
        out_shape=[jax.ShapeDtypeStruct((rows, cq), BF16), jax.ShapeDtypeStruct((rows, ck), BF16)],
        in_specs=[VM, VM, HB, HB] + [VM] * 4,
        out_specs=[VM, VM],
        scratch_shapes=[
            pltpu.VMEM((rows, width), BF16),
            pltpu.VMEM(wq.shape[1:], BF16),
            pltpu.VMEM(wkv.shape[1:], BF16),
            dma(2),
            dma(2, rows // PIECE),
            dma(2, rows // PIECE),
        ],
        compiler_params=parameters(number),
        name="gather_project",
    )(tokens, gain, wq, wkv, *tables)


def exchange(n, layer, number, x, w, rest, gain, after, tables=None):
    rows, width = x.shape[0], w.shape[2]
    half = rows // 2
    wide = tables is None
    count = half // CHUNK
    if wide:
        outs = [jax.ShapeDtypeStruct((rows, after[0].shape[2]), BF16)]
        kept = [pltpu.VMEM(after[0].shape, BF16)]
    else:
        outs = [jax.ShapeDtypeStruct((rows, part.shape[2]), BF16) for part in after]
        kept = [pltpu.VMEM(part.shape[1:], BF16) for part in after]
    outs.append(jax.ShapeDtypeStruct((half, width), F32))
    more = () if wide else tables
    return pl.pallas_call(
        functools.partial(exchange_kernel, n, layer, wide),
        out_shape=outs,
        in_specs=[VM, HB, VM, VM] + [HB] * len(after) + [VM] * len(more),
        out_specs=[VM] * len(outs),
        scratch_shapes=[
            pltpu.VMEM((rows, width), F32),
            pltpu.VMEM((rows, width), BF16),
            pltpu.VMEM((rows, width), BF16),
            pltpu.VMEM((rows, width), BF16),
            pltpu.VMEM(w.shape[1:], BF16),
            *kept,
            dma(3),
            dma(2, count),
            dma(2, count),
            dma(2, count),
            dma(2, count),
        ],
        compiler_params=parameters(number),
        name="exchange",
    )(x, w, rest, gain, *after, *more)


def scatter(n, layer, number, x, w, rest):
    rows, width = x.shape[0], w.shape[2]
    return pl.pallas_call(
        functools.partial(scatter_kernel, n, layer),
        out_shape=jax.ShapeDtypeStruct((rows // n, width), F32),
        in_specs=[VM, HB, VM],
        out_specs=VM,
        scratch_shapes=[
            pltpu.VMEM((rows, width), F32),
            pltpu.VMEM((2, rows, width), BF16),
            pltpu.VMEM((2, rows, width), BF16),
            pltpu.VMEM(w.shape[1:], BF16),
            dma(1),
            dma(2, rows // CHUNK),
            dma(2, rows // CHUNK),
        ],
        compiler_params=parameters(number),
        name="scatter",
    )(x, w, rest)


def lane_tables():
    freq = 500000.0 ** (-(np.arange(HD // 2) * 2.0 / HD))
    angle = np.arange(SEG_LEN)[:, None] * freq[None, :]
    c, s = np.cos(angle), np.sin(angle)
    cosine, sine = np.concatenate([c, c], 1), np.concatenate([-s, s], 1)
    tables = (
        np.concatenate([cosine, cosine], 1),
        np.concatenate([sine, sine], 1),
        np.concatenate([cosine, np.ones_like(cosine)], 1),
        np.concatenate([sine, np.zeros_like(sine)], 1),
    )
    return tuple(jnp.asarray(table, F32) for table in tables)


def heads_dot(a, b):
    return lax.dot_general(a, b, (((1,), (1,)), ((), ())), preferred_element_type=F32)


def attend_kernel(count, query, pairs, slots, bias, initial, weight, keep, rate, out, after,
                  written, box, probs, state, send, recv):
    me = lax.axis_index("seg")
    group = HEADS // KV_HEADS
    local_kv = pairs.shape[1] // (2 * HD)
    span = group * HD
    scale = HD ** (-0.5)
    barrier = pltpu.get_barrier_semaphore()

    def greet(k, carry):
        @pl.when(k != me)
        def _():
            pl.semaphore_signal(barrier, inc=1, device_id={"seg": k}, device_id_type=MESH)

        return carry

    lax.fori_loop(0, count, greet, 0)

    for g in range(local_kv):
        keys = pairs[:, 2 * g * HD : (2 * g + 1) * HD]
        values = pairs[:, (2 * g + 1) * HD : (2 * g + 2) * HD]
        stacked = jnp.concatenate(
            [slots[:, g * span + h * HD : g * span + (h + 1) * HD] for h in range(group)], axis=0
        )
        scores = heads_dot(stacked, keys) * scale
        top = jnp.exp(scores - jnp.max(scores, axis=-1, keepdims=True))
        share = (top / jnp.sum(top, axis=-1, keepdims=True)).astype(BF16)
        fresh = jnp.dot(share, values, preferred_element_type=F32)
        written[:, g * span : (g + 1) * span] = jnp.concatenate(
            [fresh[h * MEM : (h + 1) * MEM] for h in range(group)], axis=1
        )
    box[me] = written[...].astype(BF16)
    pl.semaphore_wait(barrier, count - 1)

    def hop(source, target):
        return pltpu.make_async_remote_copy(
            src_ref=box.at[source],
            dst_ref=box.at[source],
            send_sem=send.at[target],
            recv_sem=recv.at[source],
            device_id={"seg": target},
            device_id_type=MESH,
        )

    def post(k, carry):
        @pl.when(k > me)
        def _():
            hop(me, k).start()

        return carry

    lax.fori_loop(0, count, post, 0)
    blocks = query.shape[0] // BLOCK
    for g in range(local_kv):
        for b in range(blocks):
            rows, reach = slice(b * BLOCK, (b + 1) * BLOCK), (b + 1) * BLOCK
            parts = [
                query[rows, g * span + h * HD : g * span + (h + 1) * HD] for h in range(group)
            ]
            slot_scores = jnp.concatenate(
                [
                    heads_dot(parts[h], slots[:, g * span + h * HD : g * span + (h + 1) * HD])
                    for h in range(group)
                ],
                axis=0,
            ) * scale
            shade = bias[rows, :reach]
            token_scores = heads_dot(
                jnp.concatenate(parts, axis=0), pairs[:reach, 2 * g * HD : (2 * g + 1) * HD]
            ) * scale + jnp.concatenate([shade] * group, axis=0)
            peak = jnp.maximum(
                jnp.max(slot_scores, axis=-1, keepdims=True),
                jnp.max(token_scores, axis=-1, keepdims=True),
            )
            slot_top = jnp.exp(slot_scores - peak)
            token_top = jnp.exp(token_scores - peak)
            total = jnp.sum(slot_top, axis=-1, keepdims=True) + jnp.sum(
                token_top, axis=-1, keepdims=True
            )
            inverse = 1.0 / total
            probs[g, b, :, :MEM] = (slot_top * inverse).astype(BF16)
            probs[g, b, :, MEM : MEM + reach] = (token_top * inverse).astype(BF16)
    state[...] = keep[...] * initial[...]

    def take(k, carry):
        @pl.when(k < me)
        def _():
            hop(k, me).wait_recv()
            state[...] += weight[k] * box[k].astype(F32)

        return carry

    lax.fori_loop(0, count, take, 0)
    after[...] = rate[...] * state[...] + (1.0 - rate[...]) * written[...]
    for g in range(local_kv):
        memory = state[:, g * span : (g + 1) * span].astype(BF16)
        for b in range(blocks):
            reach = (b + 1) * BLOCK
            found = jnp.dot(
                probs[g, b, :, MEM : MEM + reach],
                pairs[:reach, (2 * g + 1) * HD : (2 * g + 2) * HD],
                preferred_element_type=F32,
            )
            pieces = [
                found[h * BLOCK : (h + 1) * BLOCK]
                + jnp.dot(
                    probs[g, b, h * BLOCK : (h + 1) * BLOCK, :MEM],
                    memory[:, h * HD : (h + 1) * HD],
                    preferred_element_type=F32,
                )
                for h in range(group)
            ]
            out[b * BLOCK : (b + 1) * BLOCK, g * span : (g + 1) * span] = jnp.concatenate(
                pieces, axis=1
            ).astype(BF16)

    def drain(k, carry):
        @pl.when(k > me)
        def _():
            hop(me, k).wait_send()

        return carry

    lax.fori_loop(0, count, drain, 0)


def attend(count, number, query, pairs, slots, bias, initial, weight, keep, rate):
    rows, columns = query.shape
    local_kv = pairs.shape[1] // (2 * HD)
    group = HEADS // KV_HEADS
    return pl.pallas_call(
        functools.partial(attend_kernel, count),
        out_shape=[
            jax.ShapeDtypeStruct((rows, columns), BF16),
            jax.ShapeDtypeStruct((MEM, columns), F32),
        ],
        in_specs=[VM] * 8,
        out_specs=[VM, VM],
        scratch_shapes=[
            pltpu.VMEM((MEM, columns), F32),
            pltpu.VMEM((count, MEM, columns), BF16),
            pltpu.VMEM((local_kv, rows // BLOCK, group * BLOCK, MEM + rows), BF16),
            pltpu.VMEM((MEM, columns), F32),
            dma(count),
            dma(count),
        ],
        compiler_params=parameters(number),
        name="attend",
    )(query, pairs, slots, bias, initial, weight, keep, rate)


def carry_weights(retain):
    count, here = lax.axis_size("seg"), lax.axis_index("seg")
    rates = lax.all_gather(retain[:, 0], "seg")
    at = jnp.arange(count)
    between = (at[None, :] > at[:, None]) & (at[None, :] < here)
    keep = jnp.prod(jnp.where(between[:, :, None, None], rates[None], 1.0), axis=1)
    weight = jnp.where((at < here)[:, None, None], (1.0 - rates) * keep, 0.0)
    whole = jnp.prod(jnp.where((at < here)[:, None, None], rates, 1.0), axis=0)
    weight = jnp.repeat(weight.transpose(1, 0, 2), HD, axis=2)[:, :, None, :]
    return weight, jnp.repeat(whole, HD, axis=1)[:, None, :], jnp.repeat(retain, HD, axis=2)


def body(
    tokens,
    document_index,
    block_mask,
    slot_keys,
    mem_init,
    retain,
    attn_gain,
    mlp_gain,
    w_query,
    w_kv,
    w_out,
    w_gate_up,
    w_down,
):
    n, count = lax.axis_size("head"), lax.axis_size("seg")
    tables = lane_tables()
    weight, keep, rate = carry_weights(retain)
    causal = jnp.arange(SEG_LEN)[:, None] >= jnp.arange(SEG_LEN)[None, :]
    blocks = jnp.repeat(jnp.repeat(block_mask[0], BLOCK, axis=0), BLOCK, axis=1)
    same = document_index[:, None] == document_index[None, :]
    bias = jnp.where(causal & same & (blocks == 1), 0.0, -jnp.inf).astype(F32)
    query, pairs = gather_project(n, 0, 0, tokens, attn_gain[:1], w_query, w_kv, tables)
    rest = tokens
    stored = []
    for layer in range(DEPTH_NUMBER):
        attended, after = attend(
            count, 5 + layer, query, pairs, slot_keys[layer], bias, mem_init[layer],
            weight[layer], keep[layer], rate[layer],
        )
        stored.append(after)
        widening = jnp.swapaxes(w_gate_up[layer], 0, 1)
        inner, rest = exchange(
            n, layer, 1 + 2 * layer, attended, w_out, rest, mlp_gain[layer : layer + 1], (widening,)
        )
        if layer + 1 < DEPTH_NUMBER:
            query, pairs, rest = exchange(
                n, layer, 2 + 2 * layer, inner, w_down, rest, attn_gain[layer + 1 : layer + 2],
                (w_query, w_kv), tables,
            )
        else:
            stream = scatter(n, layer, 2 + 2 * layer, inner, w_down, rest)
    return (stream, jnp.stack(stored)[:, None])


def solution(mesh):
    return jax.shard_map(
        body,
        mesh=mesh,
        in_specs=(
            P(("seg", "head"), None),
            P("seg"),
            P("seg", None, None),
            P(None, None, "head"),
            P(None, None, "head"),
            P(None, "seg", "head"),
            P(),
            P(),
            P(None, None, "head"),
            P(None, None, "head"),
            P(None, "head", None),
            P(None, None, None, "head"),
            P(None, "head", None),
        ),
        out_specs=(P(("seg", "head"), None), P(None, "seg", None, "head")),
        check_vma=False,
    )
```
